32 devices in a mesh: tx: 4 (over z), ty: 8 (over y, x, core).
Axes of the slice: x: 2, y: 2, z: 4, core: 2. Of those that a mesh axis runs over, the one named last changes fastest.
Arguments:
- object_init: float32 [4, 1024, 2048], P(None, 'tx', 'ty'), may hold values from -5 to 5
- probe: float32 [2, 128, 128], replicated, may hold values from -4 to 4
- propagator_phase: float32 [128, 128], replicated, may hold values from -3.140625 to 3.140625
- measured: bfloat16 [4, 8, 8, 2, 128, 128], P('tx', 'ty'), may hold values from 0 to 1.5
- corners: int32 [4, 8, 16, 2], P('tx', 'ty'), may hold values from 0 to 128
- owner_column: int32 [4, 8, 16, 1], P('tx', 'ty'), may hold values from 0 to 7; in each aligned block of 16 rows (0 to 15, 16 to 31, ..., all dimensions but the last counted through in order) at most 2 rows name the same one
Outputs:
- object_final: float32 [4, 1024, 2048], P(None, 'tx', 'ty')
The draws below stay inside these ranges and needn't reach their ends.
Inputs may be any that keep to these rules, and one draw needn't show every extreme that they name: `owner_column`: at most 2 of the 16 positions of one tile name the same owner column.
All inputs are finite; a program needn't handle non-finite values.
Results may differ from the reference program's by a relative error of at most 0.0049.
Values may be sent and summed in bfloat16 or wider, within the bound.
A program may use at most 128 MiB of HBM per device.

```python
import math
import jax
import jax.numpy as jnp
import numpy as np
from jax import lax

WINDOW = 128
SLICES = 2
TILE = 256
PATCH_DEV = 16
CAP = 2
ITERS = 1
NR = 1024
NC = 2048
N_TX = 4
N_TY = 8


def set_ends(array, own_key, low, high):
    index_at = [jax.random.randint(jax.random.fold_in(own_key, axis), (), 0, length) for axis, length in enumerate(array.shape)]
    longest = array.shape.index(max(array.shape))
    beside = index_at[:longest] + [(index_at[longest] + 1) % array.shape[longest]] + index_at[longest + 1:]
    return array.at[tuple(index_at)].set(low).at[tuple(beside)].set(high)


def block_levels(stream_key, shape, split, least, largest):
    def one(position, blocks):
        heights = jax.random.uniform(jax.random.fold_in(jax.random.fold_in(stream_key, 6), position), (blocks,), jnp.float32, least / len(split), largest / len(split))
        return jnp.repeat(jnp.exp(heights), shape[position] // blocks).reshape((-1,) + (1,) * (len(shape) - position - 1))

    level = one(*split[0])
    for cut in split[1:]:
        level = level * one(*cut)
    return level


def routed_block(rng, own, number, rows, count, top, bound, slope):
    ranking = jax.random.permutation(rng, count)
    crowded, ordinary = shares(count, rows * top, bound, slope, True), shares(count, rows * top, bound, slope, False)
    places = jnp.arange(count)

    def named(sizes, turn):
        used = int((sizes > 0).sum())
        fixed = max(1, used // 4)
        moved = fixed + (places - fixed + turn * (used - fixed)) % max(1, count - fixed)
        return jnp.zeros((count,), jnp.int32).at[ranking[jnp.where(places < fixed, places, moved)]].set(jnp.asarray(sizes, jnp.int32))

    sizes = jnp.where(number % 4 == 0, named(crowded, number // 4), named(ordinary, number - number // 4 - 1))
    mixed = jax.random.permutation(jax.random.fold_in(own, 3), count)
    giver, taker = mixed[0:count // 2 * 2:2], mixed[1:count // 2 * 2:2]
    room = jnp.minimum(sizes[giver] - 1, bound - sizes[taker]) // 2
    room = jnp.where((giver == ranking[0]) | (taker == ranking[0]) | (sizes[taker] == 0), 0, jnp.maximum(room, 0))
    moved = jax.random.randint(jax.random.fold_in(own, 4), (count // 2,), 0, 1 << 20) % (room + 1)
    sizes = sizes.at[giver].add(-moved).at[taker].add(moved)
    members = jnp.searchsorted(jnp.cumsum(sizes), jnp.arange(rows * top), side="right").astype(jnp.int32)
    table = members.reshape(top, rows).T
    table = table[jax.random.permutation(jax.random.fold_in(own, 1), rows)]
    turn = jax.random.randint(jax.random.fold_in(own, 2), (rows, 1), 0, top)
    return jnp.take_along_axis(table, (jnp.arange(top)[None, :] + turn) % top, axis=1)


def shares(amount, total, most, slope, full):
    loads = [(1 << 20) // math.isqrt(rank ** slope) + 1 for rank in range(1, amount + 1)]
    largest = most if full else min(most, max(-(-total // amount), total * loads[0] // sum(loads)))
    least = 1 if total - largest >= amount - 1 else 0
    given, spare = [largest] + [least] * (amount - 1), total - largest - least * (amount - 1)
    while spare > 0:
        free = [i for i in range(1, amount) if given[i] < largest] or [i for i in range(1, amount) if given[i] < most]
        pool, remaining = sum([loads[i] for i in free]), spare
        for i in free:
            addition = min(most - given[i], max(1, remaining * loads[i] // pool), spare)
            given[i] = given[i] + addition
            spare = spare - addition
    return np.array(given)


def bell_draw(rng, shape, scale, most, split=(), held_as=jnp.bfloat16):
    entries = scale * jax.random.normal(rng, shape, jnp.float32)
    if split:
        entries = entries * block_levels(rng, shape, split, -0.22, 0.18)
    return jnp.clip(entries, -most, most).astype(held_as)


def setup_inputs(seed: int = 0) -> dict:
    splits = jax.random.split(jax.random.key(seed), 7)
    object_init = bell_draw(splits[0], (2 * SLICES, NR, NC), 0.7, 5.0, ((1, 4), (2, 8)), jnp.float32)
    probe = bell_draw(splits[1], (2, WINDOW, WINDOW), 0.5, 4.0, (), jnp.float32)
    propagator_phase = jnp.clip(jax.random.uniform(splits[2], (WINDOW, WINDOW), jnp.float32, -3.140625, 3.140625), -3.140625, 3.140625)
    measured = jnp.clip(1.5 * jax.random.uniform(splits[3], (N_TX, N_TY, N_TY, CAP, WINDOW, WINDOW), jnp.float32) ** block_levels(splits[3], (N_TX, N_TY, N_TY, CAP, WINDOW, WINDOW), ((0, 4), (1, 8)), -0.2, 0.2), 0.0, 1.5).astype(jnp.bfloat16)
    corners = set_ends(jax.random.randint(splits[4], (N_TX, N_TY, PATCH_DEV, 2), 0, TILE - WINDOW + 1), jax.random.fold_in(splits[4], 1), 0, TILE - WINDOW).astype(jnp.int32)
    owner_column_keys = jax.random.split(jax.random.fold_in(splits[5], 1), N_TX * N_TY * PATCH_DEV // PATCH_DEV)
    owner_column_turns = jax.random.permutation(jax.random.fold_in(splits[5], 3), N_TX * N_TY * PATCH_DEV // PATCH_DEV)
    owner_column = jax.vmap(lambda own, number: routed_block(jax.random.fold_in(splits[5], 2), own, number, PATCH_DEV, N_TY, 1, CAP, 2))(owner_column_keys, owner_column_turns).reshape((N_TX, N_TY, PATCH_DEV, 1))
    return {"object_init": object_init, "probe": probe, "propagator_phase": propagator_phase, "measured": measured, "corners": corners, "owner_column": owner_column}


exact = lax.Precision.HIGHEST
step_rate = 0.5
smooth_rate = 0.2

def dft_tables(width):
    index = jnp.arange(width)
    product = index[:, None] * index[None, :] % width
    angles = product.astype(jnp.float32) * (2.0 * math.pi / width)
    scale = 1.0 / math.sqrt(width)
    return (jnp.cos(angles) * scale, jnp.sin(angles) * scale)

def left_apply(matrix, field):
    return jnp.einsum('ij,...jk->...ik', matrix, field, precision=exact)

def right_apply(field, matrix):
    return jnp.einsum('...ij,jk->...ik', field, matrix, precision=exact)

def transform(pair, cosine, sine, sign):
    real_part, imag_part = pair
    imag_table = sign * sine
    left_real = left_apply(cosine, real_part) - left_apply(imag_table, imag_part)
    left_imag = left_apply(cosine, imag_part) + left_apply(imag_table, real_part)
    return (right_apply(left_real, cosine) - right_apply(left_imag, imag_table), right_apply(left_real, imag_table) + right_apply(left_imag, cosine))

def times_complex(first, second):
    return (first[0] * second[0] - first[1] * second[1], first[0] * second[1] + first[1] * second[0])

def conjugate_times(first, second):
    return (first[0] * second[0] + first[1] * second[1], first[0] * second[1] - first[1] * second[0])

def window_gradients(windows, amplitude, probe, phase, cosine, sine):
    slices = windows.shape[1] // 2
    layers = [(windows[:, 2 * layer], windows[:, 2 * layer + 1]) for layer in range(slices)]
    probe_pair = (probe[0], probe[1])
    kernel = (jnp.cos(phase), jnp.sin(phase))
    kernel_conj = (kernel[0], -kernel[1])

    def propagate(field, factor):
        spectrum = transform(field, cosine, sine, -1.0)
        return transform(times_complex(factor, spectrum), cosine, sine, 1.0)
    wave = times_complex(probe_pair, layers[0])
    incoming = []
    for layer in range(1, slices):
        moved = propagate(wave, kernel)
        incoming.append(moved)
        wave = times_complex(layers[layer], moved)
    far_field = transform(wave, cosine, sine, -1.0)
    magnitude = jnp.sqrt(far_field[0] * far_field[0] + far_field[1] * far_field[1] + 1.0)
    factor = 1.0 - amplitude / magnitude
    back = transform((far_field[0] * factor, far_field[1] * factor), cosine, sine, 1.0)
    grads = [None] * slices
    for layer in range(slices - 1, 0, -1):
        grads[layer] = conjugate_times(incoming[layer - 1], back)
        back = propagate(conjugate_times(layers[layer], back), kernel_conj)
    grads[0] = conjugate_times(probe_pair, back)
    return jnp.stack([part for pair in grads for part in pair], axis=1)

def slot_table(owner):
    order = jnp.arange(owner.shape[0])
    same = owner[:, None] == owner[None, :]
    earlier = order[None, :] < order[:, None]
    return lax.optimization_barrier(jnp.sum(jnp.where(same & earlier, 1, 0), axis=1)).astype(jnp.int32)

def smooth_padded(padded):
    center = padded[:, 1:-1, 1:-1]
    views = [padded[:, 2:, 1:-1], padded[:, :-2, 1:-1], padded[:, 1:-1, 2:], padded[:, 1:-1, :-2]]
    slices = center.shape[0] // 2
    total = jnp.zeros_like(center)
    for view in views:
        pairs = (view - center).reshape((slices, 2) + center.shape[1:])
        weight = 1.0 / jnp.sqrt(1.0 + pairs[:, 0] * pairs[:, 0] + pairs[:, 1] * pairs[:, 1])
        total = total + (pairs * weight[:, None]).reshape(center.shape)
    return center + smooth_rate * total

def accumulate(total, grads, tops, lefts):
    zero_index = jnp.zeros((), jnp.int32)

    def add_one(index, acc):
        piece = grads[index].astype(jnp.float32)
        start = (zero_index, tops[index].astype(jnp.int32), lefts[index].astype(jnp.int32))
        current = lax.dynamic_slice(acc, start, piece.shape)
        return lax.dynamic_update_slice(acc, current + piece, start)
    return lax.fori_loop(0, grads.shape[0], add_one, total)

def reference(object_init, probe, propagator_phase, measured, corners, owner_column):
    cosine, sine = dft_tables(WINDOW)
    field = object_init
    channels = field.shape[0]
    zero_index = jnp.zeros((), jnp.int32)
    for iteration in range(ITERS):

        def tile_step(index, total):
            index = jnp.asarray(index).astype(jnp.int32)
            row_tile = index // N_TY
            col_tile = index % N_TY
            tops = (corners[row_tile, col_tile, :, 0] + row_tile * TILE).astype(jnp.int32)
            lefts = (corners[row_tile, col_tile, :, 1] + col_tile * TILE).astype(jnp.int32)
            windows = jax.vmap(lambda top, left: lax.dynamic_slice(field, (zero_index, top, left), (channels, WINDOW, WINDOW)))(tops, lefts)
            windows = windows.astype(jnp.bfloat16)
            owner = owner_column[row_tile, col_tile, :, 0]
            slot = slot_table(owner)
            amplitude = measured[row_tile, owner, col_tile, slot]
            grads = window_gradients(windows.astype(jnp.float32), amplitude.astype(jnp.float32), probe, propagator_phase, cosine, sine)
            return accumulate(total, grads.astype(jnp.bfloat16), tops, lefts)
        total = lax.fori_loop(0, N_TX * N_TY, tile_step, jnp.zeros(field.shape, jnp.float32))
        updated = field - step_rate * total
        field = smooth_padded(jnp.pad(updated, ((0, 0), (1, 1), (1, 1))))
    return field
```

```python
import functools
import math

import jax
import jax.numpy as jnp
import numpy as np
from jax import lax
from jax.experimental import pallas as pl
from jax.experimental.pallas import tpu as pltpu
from jax.sharding import PartitionSpec as P

step_rate = 0.5
smooth_rate = 0.2
group = 4


def dft_blocks(width):
    index = np.arange(width)
    angles = (index[:, None] * index[None, :] % width) * (2.0 * math.pi / width)
    cosine = np.cos(angles) / math.sqrt(width)
    sine = np.sin(angles) / math.sqrt(width)
    blocks = [
        np.block([[cosine, sine], [-sine, cosine]]).astype(np.float32),
        np.block([[cosine, -sine], [sine, cosine]]).astype(np.float32),
    ]
    parts = []
    for block in blocks:
        head = block.astype(jnp.bfloat16)
        parts += [head, (block - head.astype(np.float32)).astype(jnp.bfloat16)]
    return jnp.asarray(np.stack(parts))


def times(a, b):
    return (a[0] * b[0] - a[1] * b[1], a[0] * b[1] + a[1] * b[0])


def conj_times(a, b):
    return (a[0] * b[0] + a[1] * b[1], a[0] * b[1] - a[1] * b[0])


def dot(a, b):
    return jnp.dot(a, b, preferred_element_type=jnp.float32)


def transform_two(first, second, left, right, width):
    field = jnp.concatenate(
        [
            jnp.concatenate([first[0], second[0]], axis=1),
            jnp.concatenate([first[1], second[1]], axis=1),
        ],
        axis=0,
    ).astype(jnp.bfloat16)
    y = (dot(left[0], field) + dot(left[1], field)).astype(jnp.bfloat16)
    turned = jnp.concatenate(
        [
            jnp.concatenate([y[:width, :width], y[width:, :width]], axis=1),
            jnp.concatenate([y[:width, width:], y[width:, width:]], axis=1),
        ],
        axis=0,
    )
    z = dot(turned, right[0]) + dot(turned, right[1])
    return (
        (z[:width, :width], z[:width, width:]),
        (z[width:, :width], z[width:, width:]),
    )


def transform(fields, tables, inverse, width):
    a, b = (tables[0], tables[1]), (tables[2], tables[3])
    left, right = (b, a) if inverse else (a, b)
    out = []
    for i in range(0, len(fields), 2):
        out += transform_two(fields[i], fields[i + 1], left, right, width)
    return out


def forward(step, refs, scratch, width):
    corners, obj, probe, tables = refs
    h_ref, t1_ref, p_ref, inc_ref, far_ref = scratch
    rows = lax.broadcasted_iota(jnp.int32, (width, width), 0)
    cols = lax.broadcasted_iota(jnp.int32, (width, width), 1)
    h = (h_ref[0], h_ref[1])
    t0s, t1s, ps = [], [], []
    for j in range(group):
        k = step * group + j
        top, left = corners[k, 0], corners[k, 1]
        low_r, low_c = rows >= top, cols >= left

        def cells(ch):
            upper = jnp.where(low_c, obj[ch, :width, :width], obj[ch, :width, width:])
            lower = jnp.where(low_c, obj[ch, width:, :width], obj[ch, width:, width:])
            return jnp.where(low_r, upper, lower).astype(jnp.bfloat16).astype(jnp.float32)

        def turned(ch):
            moved = pltpu.roll(probe[ch], lax.rem(top, width), 0)
            return pltpu.roll(moved, lax.rem(left, width), 1)

        t0s.append((cells(0), cells(1)))
        t1s.append((cells(2), cells(3)))
        ps.append((turned(0), turned(1)))
    wave = [times(p, t) for p, t in zip(ps, t0s)]
    spectrum = transform(wave, tables, False, width)
    inc = transform([times(h, s) for s in spectrum], tables, True, width)
    far = transform([times(t, w) for t, w in zip(t1s, inc)], tables, False, width)
    for j in range(group):
        k = step * group + j
        for c in range(2):
            t1_ref[k, c] = t1s[j][c]
            p_ref[k, c] = ps[j][c]
            inc_ref[k, c] = inc[j][c]
            far_ref[k, c] = far[j][c]


def backward(step, entries, amp, tables, scratch, grads, width):
    h_ref, t1_ref, p_ref, inc_ref, far_ref = scratch
    h = (h_ref[0], h_ref[1])
    damped, t1s = [], []
    for j in range(group):
        k = step * group + j
        far = (far_ref[k, 0], far_ref[k, 1])
        value = amp[entries(k)].astype(jnp.float32)
        factor = 1.0 - value * lax.rsqrt(far[0] * far[0] + far[1] * far[1] + 1.0)
        damped.append((far[0] * factor, far[1] * factor))
        t1s.append((t1_ref[k, 0], t1_ref[k, 1]))
    back = transform(damped, tables, True, width)
    for j in range(group):
        k = step * group + j
        g = conj_times((inc_ref[k, 0], inc_ref[k, 1]), back[j])
        grads[k, 2] = g[0].astype(jnp.bfloat16)
        grads[k, 3] = g[1].astype(jnp.bfloat16)
    spectrum = transform(
        [conj_times(t, w) for t, w in zip(t1s, back)], tables, False, width
    )
    back = transform([conj_times(h, s) for s in spectrum], tables, True, width)
    for j in range(group):
        k = step * group + j
        g = conj_times((p_ref[k, 0], p_ref[k, 1]), back[j])
        grads[k, 0] = g[0].astype(jnp.bfloat16)
        grads[k, 1] = g[1].astype(jnp.bfloat16)


def gather_add(block, corners, obj, grads, out, width):
    count, channels = grads.shape[:2]
    start = pl.multiple_of(block * 16, 16)
    rows = lax.broadcasted_iota(jnp.int32, (16, width), 0) + start
    cols = lax.broadcasted_iota(jnp.int32, (16, width), 1)
    totals = [[jnp.zeros((16, width), jnp.float32)] * 4 for _ in range(channels)]
    for k in range(count):
        low_r, low_c = rows >= corners[k, 0], cols >= corners[k, 1]
        for ch in range(channels):
            g = grads[k, ch, pl.ds(start, 16), :].astype(jnp.float32)
            upper = jnp.where(low_r, g, 0.0)
            lower = g - upper
            upper_left = jnp.where(low_c, upper, 0.0)
            lower_left = jnp.where(low_c, lower, 0.0)
            t = totals[ch]
            totals[ch] = [
                t[0] + upper_left,
                t[1] + (upper - upper_left),
                t[2] + lower_left,
                t[3] + (lower - lower_left),
            ]
    for ch in range(channels):
        for part in range(4):
            at = pl.ds(pl.multiple_of(start + (part // 2) * width, 16), 16)
            side = pl.ds((part % 2) * width, width)
            out[ch, at, side] = obj[ch, at, side] - step_rate * totals[ch][part]


def tile_edges(upd, edges):
    channels, size = upd.shape[0], upd.shape[1]
    for ch in range(channels):
        edges[0, ch : ch + 1, :] = upd[ch, 0:1, :]
        edges[1, ch : ch + 1, :] = upd[ch, size - 1 : size, :]
        edges[2, ch : ch + 1, :] = upd[ch, :, 0:128].T[0:1, :]
        edges[3, ch : ch + 1, :] = upd[ch, :, size - 128 :].T[127:128, :]


def smooth(upd, above, below, before, after, out):
    channels, size = upd.shape[0], upd.shape[1]
    rows = lax.broadcasted_iota(jnp.int32, (size, size), 0)
    cols = lax.broadcasted_iota(jnp.int32, (size, size), 1)

    def column(row):
        return jnp.broadcast_to(row, (128, size)).T[:, 0:1]

    for s in range(channels // 2):
        pair = (2 * s, 2 * s + 1)
        v = [upd[ch] for ch in pair]
        up = [jnp.where(rows == 0, above[ch : ch + 1, :], pltpu.roll(x, 1, 0)) for ch, x in zip(pair, v)]
        down = [
            jnp.where(rows == size - 1, below[ch : ch + 1, :], pltpu.roll(x, size - 1, 0))
            for ch, x in zip(pair, v)
        ]
        left = [
            jnp.where(cols == 0, column(before[ch : ch + 1, :]), pltpu.roll(x, 1, 1))
            for ch, x in zip(pair, v)
        ]
        right = [
            jnp.where(cols == size - 1, column(after[ch : ch + 1, :]), pltpu.roll(x, size - 1, 1))
            for ch, x in zip(pair, v)
        ]
        total = [jnp.zeros_like(v[0]), jnp.zeros_like(v[0])]
        for view in (up, down, left, right):
            d = [view[0] - v[0], view[1] - v[1]]
            weight = lax.rsqrt(1.0 + d[0] * d[0] + d[1] * d[1])
            total = [total[0] + d[0] * weight, total[1] + d[1] * weight]
        for ch, x, t in zip(pair, v, total):
            out[ch] = x + smooth_rate * t


def step_kernel(
    corners, owner, obj, probe, phase, table_ref, amp, upd, edges,
    h_ref, t1_ref, p_ref, inc_ref, far_ref, grads,
):
    width, count = probe.shape[-1], corners.shape[0]
    scratch = (h_ref, t1_ref, p_ref, inc_ref, far_ref)
    h_ref[0] = jnp.cos(phase[...])
    h_ref[1] = jnp.sin(phase[...])
    tables = [table_ref.at[i] for i in range(4)]

    def entry(k):
        mine = owner[k]

        def same(i, n):
            return n + jnp.where((owner[i] == mine) & (i < k), 1, 0)

        slot = lax.fori_loop(0, count, same, jnp.int32(0), unroll=True)
        return mine, slot

    @pl.loop(0, count // group)
    def _(step):
        forward(step, (corners, obj, probe, [t[...] for t in tables]), scratch, width)

    @pl.loop(0, count // group)
    def _(step):
        backward(step, entry, amp, [t[...] for t in tables], scratch, grads, width)

    @pl.loop(0, width // 16)
    def _(block):
        gather_add(block, corners, obj, grads, upd, width)

    tile_edges(upd, edges)


def smooth_kernel(upd, above, below, before, after, out):
    smooth(upd, above, below, before, after, out)


def per_device(object_init, probe, propagator_phase, measured, corners, owner_column):
    width = probe.shape[-1]
    channels, size = object_init.shape[0], object_init.shape[1]
    count = corners.shape[2]
    amp = lax.all_to_all(measured[0, 0], "ty", split_axis=0, concat_axis=0, tiled=True)
    smem = pl.BlockSpec(memory_space=pltpu.SMEM)
    vmem = pl.BlockSpec(memory_space=pltpu.VMEM)
    held = pltpu.VMEM((count, 2, width, width), jnp.float32)
    upd, edges = pl.pallas_call(
        step_kernel,
        out_shape=(
            jax.ShapeDtypeStruct(object_init.shape, jnp.float32),
            jax.ShapeDtypeStruct((4, channels, size), jnp.float32),
        ),
        in_specs=[smem, smem] + [vmem] * 5,
        out_specs=(vmem, vmem),
        scratch_shapes=[
            pltpu.VMEM((2, width, width), jnp.float32),
            held, held, held, held,
            pltpu.VMEM((count, channels, width, width), jnp.bfloat16),
        ],
        compiler_params=pltpu.CompilerParams(vmem_limit_bytes=48 * 1024 * 1024),
    )(corners[0, 0], owner_column[0, 0, :, 0], object_init, probe, propagator_phase,
      dft_blocks(width), amp)
    halos = []
    for axis, first, last in (("tx", 0, 1), ("ty", 2, 3)):
        n = lax.axis_size(axis)
        up = [(i, i + 1) for i in range(n - 1)]
        down = [(i + 1, i) for i in range(n - 1)]
        halos.append(lax.ppermute(edges[last], axis, up))
        halos.append(lax.ppermute(edges[first], axis, down))
    return pl.pallas_call(
        smooth_kernel,
        out_shape=jax.ShapeDtypeStruct(object_init.shape, jnp.float32),
        in_specs=[vmem] * 5,
        out_specs=vmem,
        compiler_params=pltpu.CompilerParams(vmem_limit_bytes=48 * 1024 * 1024),
    )(upd, *halos)


def solution(mesh):
    placed = (
        P(None, "tx", "ty"),
        P(),
        P(),
        P("tx", "ty", None, None, None, None),
        P("tx", "ty", None, None),
        P("tx", "ty", None, None),
    )
    return jax.shard_map(
        per_device, mesh=mesh, in_specs=placed, out_specs=P(None, "tx", "ty"), check_vma=False
    )
```

```python
import math

import jax
import jax.numpy as jnp
import numpy as np
from jax import lax
from jax.experimental import pallas as pl
from jax.experimental.pallas import tpu as pltpu
from jax.sharding import PartitionSpec as P

step_rate = 0.5
smooth_rate = 0.2
MESH = pl.DeviceIdType.MESH
group = 4


def dft_blocks(width):
    index = np.arange(width)
    angles = (index[:, None] * index[None, :] % width) * (2.0 * math.pi / width)
    cosine = np.cos(angles) / math.sqrt(width)
    sine = np.sin(angles) / math.sqrt(width)
    blocks = [
        np.block([[cosine, sine], [-sine, cosine]]).astype(np.float32),
        np.block([[cosine, -sine], [sine, cosine]]).astype(np.float32),
    ]
    parts = []
    for block in blocks:
        head = block.astype(jnp.bfloat16)
        parts += [head, (block - head.astype(np.float32)).astype(jnp.bfloat16)]
    return jnp.asarray(np.stack(parts))


def times(a, b):
    return (a[0] * b[0] - a[1] * b[1], a[0] * b[1] + a[1] * b[0])


def conj_times(a, b):
    return (a[0] * b[0] + a[1] * b[1], a[0] * b[1] - a[1] * b[0])


def dot(a, b):
    return jnp.dot(a, b, preferred_element_type=jnp.float32)


def transform_two(first, second, left, right, width):
    field = jnp.concatenate(
        [
            jnp.concatenate([first[0], second[0]], axis=1),
            jnp.concatenate([first[1], second[1]], axis=1),
        ],
        axis=0,
    ).astype(jnp.bfloat16)
    y = (dot(left[0], field) + dot(left[1], field)).astype(jnp.bfloat16)
    turned = jnp.concatenate(
        [
            jnp.concatenate([y[:width, :width], y[width:, :width]], axis=1),
            jnp.concatenate([y[:width, width:], y[width:, width:]], axis=1),
        ],
        axis=0,
    )
    z = dot(turned, right[0]) + dot(turned, right[1])
    return (
        (z[:width, :width], z[:width, width:]),
        (z[width:, :width], z[width:, width:]),
    )


def transform(fields, tables, inverse, width):
    a, b = (tables[0], tables[1]), (tables[2], tables[3])
    left, right = (b, a) if inverse else (a, b)
    out = []
    for i in range(0, len(fields), 2):
        out += transform_two(fields[i], fields[i + 1], left, right, width)
    return out


def forward(step, refs, scratch, width):
    corners, obj, probe, tables = refs
    h_ref, t1_ref, p_ref, inc_ref, far_ref = scratch
    rows = lax.broadcasted_iota(jnp.int32, (width, width), 0)
    cols = lax.broadcasted_iota(jnp.int32, (width, width), 1)
    h = (h_ref[0], h_ref[1])
    t0s, t1s, ps = [], [], []
    for j in range(group):
        k = step * group + j
        top, left = corners[0, k], corners[1, k]
        low_r, low_c = rows >= top, cols >= left

        def cells(ch):
            upper = jnp.where(low_c, obj[ch, :width, :width], obj[ch, :width, width:])
            lower = jnp.where(low_c, obj[ch, width:, :width], obj[ch, width:, width:])
            return jnp.where(low_r, upper, lower).astype(jnp.bfloat16).astype(jnp.float32)

        def turned(ch):
            moved = pltpu.roll(probe[ch], lax.rem(top, width), 0)
            return pltpu.roll(moved, lax.rem(left, width), 1)

        t0s.append((cells(0), cells(1)))
        t1s.append((cells(2), cells(3)))
        ps.append((turned(0), turned(1)))
    wave = [times(p, t) for p, t in zip(ps, t0s)]
    spectrum = transform(wave, tables, False, width)
    inc = transform([times(h, s) for s in spectrum], tables, True, width)
    far = transform([times(t, w) for t, w in zip(t1s, inc)], tables, False, width)
    for j in range(group):
        k = step * group + j
        for c in range(2):
            t1_ref[k, c] = t1s[j][c]
            p_ref[k, c] = ps[j][c]
            inc_ref[k, c] = inc[j][c]
            far_ref[k, c] = far[j][c]


def backward(step, entries, amp, tables, scratch, grads, width):
    h_ref, t1_ref, p_ref, inc_ref, far_ref = scratch
    h = (h_ref[0], h_ref[1])
    damped, t1s = [], []
    for j in range(group):
        k = step * group + j
        far = (far_ref[k, 0], far_ref[k, 1])
        value = amp[entries(k)].astype(jnp.float32)
        factor = 1.0 - value * lax.rsqrt(far[0] * far[0] + far[1] * far[1] + 1.0)
        damped.append((far[0] * factor, far[1] * factor))
        t1s.append((t1_ref[k, 0], t1_ref[k, 1]))
    back = transform(damped, tables, True, width)
    for j in range(group):
        k = step * group + j
        g = conj_times((inc_ref[k, 0], inc_ref[k, 1]), back[j])
        grads[k, 2] = g[0].astype(jnp.bfloat16)
        grads[k, 3] = g[1].astype(jnp.bfloat16)
    spectrum = transform(
        [conj_times(t, w) for t, w in zip(t1s, back)], tables, False, width
    )
    back = transform([conj_times(h, s) for s in spectrum], tables, True, width)
    for j in range(group):
        k = step * group + j
        g = conj_times((p_ref[k, 0], p_ref[k, 1]), back[j])
        grads[k, 0] = g[0].astype(jnp.bfloat16)
        grads[k, 1] = g[1].astype(jnp.bfloat16)


def gather_add(block, corners, obj, grads, out, width):
    count, channels = grads.shape[:2]
    start = pl.multiple_of(block * 16, 16)
    rows = lax.broadcasted_iota(jnp.int32, (16, width), 0) + start
    cols = lax.broadcasted_iota(jnp.int32, (16, width), 1)
    totals = [[jnp.zeros((16, width), jnp.float32)] * 4 for _ in range(channels)]
    for k in range(count):
        low_r, low_c = rows >= corners[0, k], cols >= corners[1, k]
        for ch in range(channels):
            g = grads[k, ch, pl.ds(start, 16), :].astype(jnp.float32)
            upper = jnp.where(low_r, g, 0.0)
            lower = g - upper
            upper_left = jnp.where(low_c, upper, 0.0)
            lower_left = jnp.where(low_c, lower, 0.0)
            t = totals[ch]
            totals[ch] = [
                t[0] + upper_left,
                t[1] + (upper - upper_left),
                t[2] + lower_left,
                t[3] + (lower - lower_left),
            ]
    for ch in range(channels):
        for part in range(4):
            at = pl.ds(pl.multiple_of(start + (part // 2) * width, 16), 16)
            side = pl.ds((part % 2) * width, width)
            out[ch, at, side] = obj[ch, at, side] - step_rate * totals[ch][part]


def tile_edges(upd, edges):
    channels, size = upd.shape[0], upd.shape[1]
    for ch in range(channels):
        edges[0, ch : ch + 1, :] = upd[ch, 0:1, :]
        edges[1, ch : ch + 1, :] = upd[ch, size - 1 : size, :]
        edges[2, ch : ch + 1, :] = upd[ch, :, 0:128].T[0:1, :]
        edges[3, ch : ch + 1, :] = upd[ch, :, size - 128 :].T[127:128, :]


def smooth(upd, above, below, before, after, out):
    channels, size = upd.shape[0], upd.shape[1]
    rows = lax.broadcasted_iota(jnp.int32, (size, size), 0)
    cols = lax.broadcasted_iota(jnp.int32, (size, size), 1)

    def column(row):
        return jnp.broadcast_to(row, (128, size)).T[:, 0:1]

    for s in range(channels // 2):
        pair = (2 * s, 2 * s + 1)
        v = [upd[ch] for ch in pair]
        up = [jnp.where(rows == 0, above[ch : ch + 1, :], pltpu.roll(x, 1, 0)) for ch, x in zip(pair, v)]
        down = [
            jnp.where(rows == size - 1, below[ch : ch + 1, :], pltpu.roll(x, size - 1, 0))
            for ch, x in zip(pair, v)
        ]
        left = [
            jnp.where(cols == 0, column(before[ch : ch + 1, :]), pltpu.roll(x, 1, 1))
            for ch, x in zip(pair, v)
        ]
        right = [
            jnp.where(cols == size - 1, column(after[ch : ch + 1, :]), pltpu.roll(x, size - 1, 1))
            for ch, x in zip(pair, v)
        ]
        total = [jnp.zeros_like(v[0]), jnp.zeros_like(v[0])]
        for view in (up, down, left, right):
            d = [view[0] - v[0], view[1] - v[1]]
            weight = lax.rsqrt(1.0 + d[0] * d[0] + d[1] * d[1])
            total = [total[0] + d[0] * weight, total[1] + d[1] * weight]
        for ch, x, t in zip(pair, v, total):
            out[ch] = x + smooth_rate * t


def step_kernel(
    corners, owner, obj_hbm, probe, phase, table_hbm, measured, out,
    obj, table_ref, amp, upd, edges, halos,
    h_ref, t1_ref, p_ref, inc_ref, far_ref, grads,
    local_sem, send_sem, recv_sem, edge_send, edge_recv,
):
    width, count = probe.shape[-1], corners.shape[1]
    columns = measured.shape[0]
    tx, ty = lax.axis_index("tx"), lax.axis_index("ty")
    tile_rows = lax.axis_size("tx")

    load_obj = pltpu.make_async_copy(obj_hbm, obj, local_sem.at[0])
    load_table = pltpu.make_async_copy(table_hbm, table_ref, local_sem.at[1])
    load_own = pltpu.make_async_copy(measured.at[ty], amp.at[ty], local_sem.at[2])
    load_obj.start()
    load_table.start()
    load_own.start()

    barrier = pltpu.get_barrier_semaphore()
    for d in range(1, columns):
        pl.semaphore_signal(
            barrier, inc=1, device_id={"ty": lax.rem(ty + d, columns)}, device_id_type=MESH
        )
    for d in (1, tile_rows - 1):
        pl.semaphore_signal(
            barrier, inc=1, device_id={"tx": lax.rem(tx + d, tile_rows)}, device_id_type=MESH
        )
    h_ref[0] = jnp.cos(phase[...])
    h_ref[1] = jnp.sin(phase[...])
    pl.semaphore_wait(barrier, columns + 1)

    sends = []
    for d in range(1, columns):
        peer = lax.rem(ty + d, columns)
        sends.append(
            pltpu.make_async_remote_copy(
                src_ref=measured.at[peer],
                dst_ref=amp.at[ty],
                send_sem=send_sem.at[d - 1],
                recv_sem=recv_sem.at[d - 1],
                device_id={"ty": peer},
                device_id_type=MESH,
            )
        )
    for send in sends:
        send.start()
    load_obj.wait()
    load_table.wait()
    scratch = (h_ref, t1_ref, p_ref, inc_ref, far_ref)
    tables = [table_ref.at[i] for i in range(4)]

    def entry(k):
        mine = owner[k]

        def same(i, n):
            return n + jnp.where((owner[i] == mine) & (i < k), 1, 0)

        slot = lax.fori_loop(0, count, same, jnp.int32(0), unroll=True)
        return mine, jnp.minimum(slot, amp.shape[1] - 1)

    @pl.loop(0, count // group)
    def _(step):
        forward(step, (corners, obj, probe, [t[...] for t in tables]), scratch, width)

    load_own.wait()
    for send in sends:
        send.wait()

    @pl.loop(0, count // group)
    def _(step):
        backward(step, entry, amp, [t[...] for t in tables], scratch, grads, width)

    @pl.loop(0, width // 16)
    def _(block):
        gather_add(block, corners, obj, grads, upd, width)

    tile_edges(upd, edges)
    moves = []
    for source, slot, device in (
        (1, 0, {"tx": lax.rem(tx + 1, tile_rows)}),
        (0, 1, {"tx": lax.rem(tx + tile_rows - 1, tile_rows)}),
        (3, 2, {"ty": lax.rem(ty + 1, columns)}),
        (2, 3, {"ty": lax.rem(ty + columns - 1, columns)}),
    ):
        moves.append(
            pltpu.make_async_remote_copy(
                src_ref=edges.at[source],
                dst_ref=halos.at[slot],
                send_sem=edge_send.at[slot],
                recv_sem=edge_recv.at[slot],
                device_id=device,
                device_id_type=MESH,
            )
        )
    for move in moves:
        move.start()
    for move in moves:
        move.wait()
    ends = (tx == 0, tx == tile_rows - 1, ty == 0, ty == columns - 1)
    smooth(upd, *[jnp.where(end, 0.0, halos[i]) for i, end in enumerate(ends)], out)


def per_device(object_init, probe, propagator_phase, measured, corners, owner_column):
    width = probe.shape[-1]
    channels, size = object_init.shape[0], object_init.shape[1]
    count = corners.shape[2]
    columns = measured.shape[2]
    smem = pl.BlockSpec(memory_space=pltpu.SMEM)
    vmem = pl.BlockSpec(memory_space=pltpu.VMEM)
    anywhere = pl.BlockSpec(memory_space=pl.ANY)
    held = pltpu.VMEM((count, 2, width, width), jnp.float32)
    tile = pltpu.VMEM((channels, size, size), jnp.float32)
    edge = pltpu.VMEM((4, channels, size), jnp.float32)
    return pl.pallas_call(
        step_kernel,
        out_shape=jax.ShapeDtypeStruct(object_init.shape, jnp.float32),
        in_specs=[smem, smem, anywhere, vmem, vmem, anywhere, anywhere],
        out_specs=vmem,
        scratch_shapes=[
            tile,
            pltpu.VMEM((4, 2 * width, 2 * width), jnp.bfloat16),
            pltpu.VMEM(measured.shape[2:], jnp.bfloat16),
            tile, edge, edge,
            pltpu.VMEM((2, width, width), jnp.float32),
            held, held, held, held,
            pltpu.VMEM((count, channels, width, width), jnp.bfloat16),
            pltpu.SemaphoreType.DMA((3,)),
            pltpu.SemaphoreType.DMA((columns - 1,)),
            pltpu.SemaphoreType.DMA((columns - 1,)),
            pltpu.SemaphoreType.DMA((4,)),
            pltpu.SemaphoreType.DMA((4,)),
        ],
        compiler_params=pltpu.CompilerParams(
            collective_id=0, has_side_effects=True, vmem_limit_bytes=60 * 1024 * 1024
        ),
    )(corners[0, 0].T, owner_column[0, 0, :, 0], object_init, probe, propagator_phase,
      dft_blocks(width), measured[0, 0])


def solution(mesh):
    placed = (
        P(None, "tx", "ty"),
        P(),
        P(),
        P("tx", "ty", None, None, None, None),
        P("tx", "ty", None, None),
        P("tx", "ty", None, None),
    )
    return jax.shard_map(
        per_device, mesh=mesh, in_specs=placed, out_specs=P(None, "tx", "ty"), check_vma=False
    )
```

```python
import math

import jax
import jax.numpy as jnp
import numpy as np
from jax import lax
from jax.experimental import pallas as pl
from jax.experimental.pallas import tpu as pltpu
from jax.sharding import PartitionSpec as P

step_rate = 0.5
smooth_rate = 0.2
MESH = pl.DeviceIdType.MESH
group = 8


def dft_blocks(width):
    index = np.arange(width)
    angles = (index[:, None] * index[None, :] % width) * (2.0 * math.pi / width)
    cosine = np.cos(angles) / math.sqrt(width)
    sine = np.sin(angles) / math.sqrt(width)
    blocks = [
        np.block([[cosine, sine], [-sine, cosine]]).astype(np.float32),
        np.block([[cosine, -sine], [sine, cosine]]).astype(np.float32),
    ]
    parts = []
    for block in blocks:
        head = block.astype(jnp.bfloat16)
        parts += [head, (block - head.astype(np.float32)).astype(jnp.bfloat16)]
    return jnp.asarray(np.stack(parts))


def times(a, b):
    return (a[0] * b[0] - a[1] * b[1], a[0] * b[1] + a[1] * b[0])


def conj_times(a, b):
    return (a[0] * b[0] + a[1] * b[1], a[0] * b[1] - a[1] * b[0])


def dot(a, b):
    return jnp.dot(a, b, preferred_element_type=jnp.float32)


def transform_two(first, second, left, right, width):
    field = jnp.concatenate(
        [
            jnp.concatenate([first[0], second[0]], axis=1),
            jnp.concatenate([first[1], second[1]], axis=1),
        ],
        axis=0,
    ).astype(jnp.bfloat16)
    y = (dot(left[0], field) + dot(left[1], field)).astype(jnp.bfloat16)
    turned = jnp.concatenate(
        [
            jnp.concatenate([y[:width, :width], y[width:, :width]], axis=1),
            jnp.concatenate([y[:width, width:], y[width:, width:]], axis=1),
        ],
        axis=0,
    )
    z = dot(turned, right[0]) + dot(turned, right[1])
    return (
        (z[:width, :width], z[:width, width:]),
        (z[width:, :width], z[width:, width:]),
    )


def transform(fields, tables, inverse, width):
    a, b = (tables[0], tables[1]), (tables[2], tables[3])
    left, right = (b, a) if inverse else (a, b)
    out = []
    for i in range(0, len(fields), 2):
        out += transform_two(fields[i], fields[i + 1], left, right, width)
    return out


def forward(step, refs, scratch, width):
    corners, obj, probe, tables = refs
    h_ref, t1_ref, p_ref, inc_ref, far_ref = scratch
    rows = lax.broadcasted_iota(jnp.int32, (width, width), 0)
    cols = lax.broadcasted_iota(jnp.int32, (width, width), 1)
    h = (h_ref[0], h_ref[1])
    t0s, t1s, ps = [], [], []
    for j in range(group):
        k = step * group + j
        top, left = corners[0, k], corners[1, k]
        low_r, low_c = rows >= top, cols >= left

        def cells(ch):
            upper = jnp.where(low_c, obj[ch, :width, :width], obj[ch, :width, width:])
            lower = jnp.where(low_c, obj[ch, width:, :width], obj[ch, width:, width:])
            return jnp.where(low_r, upper, lower).astype(jnp.bfloat16).astype(jnp.float32)

        def turned(ch):
            moved = pltpu.roll(probe[ch], lax.rem(top, width), 0)
            return pltpu.roll(moved, lax.rem(left, width), 1)

        t0s.append((cells(0), cells(1)))
        t1s.append((cells(2), cells(3)))
        ps.append((turned(0), turned(1)))
    wave = [times(p, t) for p, t in zip(ps, t0s)]
    spectrum = transform(wave, tables, False, width)
    inc = transform([times(h, s) for s in spectrum], tables, True, width)
    far = transform([times(t, w) for t, w in zip(t1s, inc)], tables, False, width)
    for j in range(group):
        k = step * group + j
        for c in range(2):
            t1_ref[k, c] = t1s[j][c]
            p_ref[k, c] = ps[j][c]
            inc_ref[k, c] = inc[j][c]
            far_ref[k, c] = far[j][c]


def backward(step, entries, amp, tables, scratch, grads, width):
    h_ref, t1_ref, p_ref, inc_ref, far_ref = scratch
    h = (h_ref[0], h_ref[1])
    damped, t1s = [], []
    for j in range(group):
        k = step * group + j
        far = (far_ref[k, 0], far_ref[k, 1])
        value = amp[entries(k)].astype(jnp.float32)
        factor = 1.0 - value * lax.rsqrt(far[0] * far[0] + far[1] * far[1] + 1.0)
        damped.append((far[0] * factor, far[1] * factor))
        t1s.append((t1_ref[k, 0], t1_ref[k, 1]))
    back = transform(damped, tables, True, width)
    for j in range(group):
        k = step * group + j
        g = conj_times((inc_ref[k, 0], inc_ref[k, 1]), back[j])
        grads[k, 2] = g[0].astype(jnp.bfloat16)
        grads[k, 3] = g[1].astype(jnp.bfloat16)
    spectrum = transform(
        [conj_times(t, w) for t, w in zip(t1s, back)], tables, False, width
    )
    back = transform([conj_times(h, s) for s in spectrum], tables, True, width)
    for j in range(group):
        k = step * group + j
        g = conj_times((p_ref[k, 0], p_ref[k, 1]), back[j])
        grads[k, 0] = g[0].astype(jnp.bfloat16)
        grads[k, 1] = g[1].astype(jnp.bfloat16)


def gather_add(block, corners, obj, grads, out, width):
    count, channels = grads.shape[:2]
    start = pl.multiple_of(block * 16, 16)
    rows = lax.broadcasted_iota(jnp.int32, (16, width), 0) + start
    cols = lax.broadcasted_iota(jnp.int32, (16, width), 1)
    totals = [[jnp.zeros((16, width), jnp.float32)] * 4 for _ in range(channels)]
    for k in range(count):
        low_r, low_c = rows >= corners[0, k], cols >= corners[1, k]
        for ch in range(channels):
            g = grads[k, ch, pl.ds(start, 16), :].astype(jnp.float32)
            upper = jnp.where(low_r, g, 0.0)
            lower = g - upper
            upper_left = jnp.where(low_c, upper, 0.0)
            lower_left = jnp.where(low_c, lower, 0.0)
            t = totals[ch]
            totals[ch] = [
                t[0] + upper_left,
                t[1] + (upper - upper_left),
                t[2] + lower_left,
                t[3] + (lower - lower_left),
            ]
    for ch in range(channels):
        for part in range(4):
            at = pl.ds(pl.multiple_of(start + (part // 2) * width, 16), 16)
            side = pl.ds((part % 2) * width, width)
            out[ch, at, side] = obj[ch, at, side] - step_rate * totals[ch][part]


def tile_edges(upd, edges):
    channels, size = upd.shape[0], upd.shape[1]
    for ch in range(channels):
        edges[0, ch : ch + 1, :] = upd[ch, 0:1, :]
        edges[1, ch : ch + 1, :] = upd[ch, size - 1 : size, :]
        edges[2, ch : ch + 1, :] = upd[ch, :, 0:128].T[0:1, :]
        edges[3, ch : ch + 1, :] = upd[ch, :, size - 128 :].T[127:128, :]


def smooth(upd, above, below, before, after, out):
    channels, size = upd.shape[0], upd.shape[1]
    rows = lax.broadcasted_iota(jnp.int32, (size, size), 0)
    cols = lax.broadcasted_iota(jnp.int32, (size, size), 1)

    def column(row):
        return jnp.broadcast_to(row, (128, size)).T[:, 0:1]

    for s in range(channels // 2):
        pair = (2 * s, 2 * s + 1)
        v = [upd[ch] for ch in pair]
        up = [jnp.where(rows == 0, above[ch : ch + 1, :], pltpu.roll(x, 1, 0)) for ch, x in zip(pair, v)]
        down = [
            jnp.where(rows == size - 1, below[ch : ch + 1, :], pltpu.roll(x, size - 1, 0))
            for ch, x in zip(pair, v)
        ]
        left = [
            jnp.where(cols == 0, column(before[ch : ch + 1, :]), pltpu.roll(x, 1, 1))
            for ch, x in zip(pair, v)
        ]
        right = [
            jnp.where(cols == size - 1, column(after[ch : ch + 1, :]), pltpu.roll(x, size - 1, 1))
            for ch, x in zip(pair, v)
        ]
        total = [jnp.zeros_like(v[0]), jnp.zeros_like(v[0])]
        for view in (up, down, left, right):
            d = [view[0] - v[0], view[1] - v[1]]
            weight = lax.rsqrt(1.0 + d[0] * d[0] + d[1] * d[1])
            total = [total[0] + d[0] * weight, total[1] + d[1] * weight]
        for ch, x, t in zip(pair, v, total):
            out[ch] = x + smooth_rate * t


def step_kernel(
    corners, owner, obj_hbm, probe, phase, table_hbm, measured, out,
    obj, table_ref, amp, upd, edges, halos,
    h_ref, t1_ref, p_ref, inc_ref, far_ref, grads,
    local_sem, send_sem, recv_sem, edge_send, edge_recv,
):
    width, count = probe.shape[-1], corners.shape[1]
    columns = measured.shape[0]
    tx, ty = lax.axis_index("tx"), lax.axis_index("ty")
    tile_rows = lax.axis_size("tx")

    load_obj = pltpu.make_async_copy(obj_hbm, obj, local_sem.at[0])
    load_table = pltpu.make_async_copy(table_hbm, table_ref, local_sem.at[1])
    load_own = pltpu.make_async_copy(measured.at[ty], amp.at[ty], local_sem.at[2])
    load_obj.start()
    load_table.start()
    load_own.start()

    barrier = pltpu.get_barrier_semaphore()
    for d in range(1, columns):
        pl.semaphore_signal(
            barrier, inc=1, device_id={"ty": lax.rem(ty + d, columns)}, device_id_type=MESH
        )
    for d in (1, tile_rows - 1):
        pl.semaphore_signal(
            barrier, inc=1, device_id={"tx": lax.rem(tx + d, tile_rows)}, device_id_type=MESH
        )
    h_ref[0] = jnp.cos(phase[...])
    h_ref[1] = jnp.sin(phase[...])
    pl.semaphore_wait(barrier, columns + 1)

    sends = []
    for d in range(1, columns):
        peer = lax.rem(ty + d, columns)
        sends.append(
            pltpu.make_async_remote_copy(
                src_ref=measured.at[peer],
                dst_ref=amp.at[ty],
                send_sem=send_sem.at[d - 1],
                recv_sem=recv_sem.at[d - 1],
                device_id={"ty": peer},
                device_id_type=MESH,
            )
        )
    for send in sends:
        send.start()
    load_obj.wait()
    load_table.wait()
    scratch = (h_ref, t1_ref, p_ref, inc_ref, far_ref)
    tables = [table_ref.at[i] for i in range(4)]

    def entry(k):
        mine = owner[k]

        def same(i, n):
            return n + jnp.where((owner[i] == mine) & (i < k), 1, 0)

        slot = lax.fori_loop(0, count, same, jnp.int32(0), unroll=True)
        return mine, jnp.minimum(slot, amp.shape[1] - 1)

    @pl.loop(0, count // group)
    def _(step):
        forward(step, (corners, obj, probe, [t[...] for t in tables]), scratch, width)

    load_own.wait()
    for send in sends:
        send.wait()

    @pl.loop(0, count // group)
    def _(step):
        backward(step, entry, amp, [t[...] for t in tables], scratch, grads, width)

    @pl.loop(0, width // 16)
    def _(block):
        gather_add(block, corners, obj, grads, upd, width)

    tile_edges(upd, edges)
    moves = []
    for source, slot, device in (
        (1, 0, {"tx": lax.rem(tx + 1, tile_rows)}),
        (0, 1, {"tx": lax.rem(tx + tile_rows - 1, tile_rows)}),
        (3, 2, {"ty": lax.rem(ty + 1, columns)}),
        (2, 3, {"ty": lax.rem(ty + columns - 1, columns)}),
    ):
        moves.append(
            pltpu.make_async_remote_copy(
                src_ref=edges.at[source],
                dst_ref=halos.at[slot],
                send_sem=edge_send.at[slot],
                recv_sem=edge_recv.at[slot],
                device_id=device,
                device_id_type=MESH,
            )
        )
    for move in moves:
        move.start()
    for move in moves:
        move.wait()
    ends = (tx == 0, tx == tile_rows - 1, ty == 0, ty == columns - 1)
    smooth(upd, *[jnp.where(end, 0.0, halos[i]) for i, end in enumerate(ends)], out)


def per_device(object_init, probe, propagator_phase, measured, corners, owner_column):
    width = probe.shape[-1]
    channels, size = object_init.shape[0], object_init.shape[1]
    count = corners.shape[2]
    columns = measured.shape[2]
    smem = pl.BlockSpec(memory_space=pltpu.SMEM)
    vmem = pl.BlockSpec(memory_space=pltpu.VMEM)
    anywhere = pl.BlockSpec(memory_space=pl.ANY)
    held = pltpu.VMEM((count, 2, width, width), jnp.float32)
    tile = pltpu.VMEM((channels, size, size), jnp.float32)
    edge = pltpu.VMEM((4, channels, size), jnp.float32)
    return pl.pallas_call(
        step_kernel,
        out_shape=jax.ShapeDtypeStruct(object_init.shape, jnp.float32),
        in_specs=[smem, smem, anywhere, vmem, vmem, anywhere, anywhere],
        out_specs=vmem,
        scratch_shapes=[
            tile,
            pltpu.VMEM((4, 2 * width, 2 * width), jnp.bfloat16),
            pltpu.VMEM(measured.shape[2:], jnp.bfloat16),
            tile, edge, edge,
            pltpu.VMEM((2, width, width), jnp.float32),
            held, held, held, held,
            pltpu.VMEM((count, channels, width, width), jnp.bfloat16),
            pltpu.SemaphoreType.DMA((3,)),
            pltpu.SemaphoreType.DMA((columns - 1,)),
            pltpu.SemaphoreType.DMA((columns - 1,)),
            pltpu.SemaphoreType.DMA((4,)),
            pltpu.SemaphoreType.DMA((4,)),
        ],
        compiler_params=pltpu.CompilerParams(
            collective_id=0, has_side_effects=True, vmem_limit_bytes=60 * 1024 * 1024
        ),
    )(corners[0, 0].T, owner_column[0, 0, :, 0], object_init, probe, propagator_phase,
      dft_blocks(width), measured[0, 0])


def solution(mesh):
    placed = (
        P(None, "tx", "ty"),
        P(),
        P(),
        P("tx", "ty", None, None, None, None),
        P("tx", "ty", None, None),
        P("tx", "ty", None, None),
    )
    return jax.shard_map(
        per_device, mesh=mesh, in_specs=placed, out_specs=P(None, "tx", "ty"), check_vma=False
    )
```

```python
import math

import jax
import jax.numpy as jnp
import numpy as np
from jax import lax
from jax.experimental import pallas as pl
from jax.experimental.pallas import tpu as pltpu
from jax.sharding import PartitionSpec as P

step_rate = 0.5
smooth_rate = 0.2
MESH = pl.DeviceIdType.MESH
group = 8


def dft_blocks(width):
    index = np.arange(width)
    angles = (index[:, None] * index[None, :] % width) * (2.0 * math.pi / width)
    cosine = np.cos(angles) / math.sqrt(width)
    sine = np.sin(angles) / math.sqrt(width)
    blocks = [
        np.block([[cosine, sine], [-sine, cosine]]).astype(np.float32),
        np.block([[cosine, -sine], [sine, cosine]]).astype(np.float32),
    ]
    parts = []
    for block in blocks:
        head = block.astype(jnp.bfloat16)
        parts += [head, (block - head.astype(np.float32)).astype(jnp.bfloat16)]
    return jnp.asarray(np.stack(parts))


def times(a, b):
    return (a[0] * b[0] - a[1] * b[1], a[0] * b[1] + a[1] * b[0])


def conj_times(a, b):
    return (a[0] * b[0] + a[1] * b[1], a[0] * b[1] - a[1] * b[0])


def dot(a, b):
    return jnp.dot(a, b, preferred_element_type=jnp.float32)


def transform_two(first, second, left, right, width):
    field = jnp.concatenate(
        [
            jnp.concatenate([first[0], second[0]], axis=1),
            jnp.concatenate([first[1], second[1]], axis=1),
        ],
        axis=0,
    ).astype(jnp.bfloat16)
    y = (dot(left[0], field) + dot(left[1], field)).astype(jnp.bfloat16)
    turned = jnp.concatenate(
        [
            jnp.concatenate([y[:width, :width], y[width:, :width]], axis=1),
            jnp.concatenate([y[:width, width:], y[width:, width:]], axis=1),
        ],
        axis=0,
    )
    z = dot(turned, right[0]) + dot(turned, right[1])
    return (
        (z[:width, :width], z[:width, width:]),
        (z[width:, :width], z[width:, width:]),
    )


def transform(fields, tables, inverse, width):
    a, b = (tables[0], tables[1]), (tables[2], tables[3])
    left, right = (b, a) if inverse else (a, b)
    out = []
    for i in range(0, len(fields), 2):
        out += transform_two(fields[i], fields[i + 1], left, right, width)
    return out


def forward(step, refs, scratch, width):
    corners, obj, probe, tables = refs
    h_ref, t1_ref, p_ref, inc_ref, far_ref = scratch
    rows = lax.broadcasted_iota(jnp.int32, (width, width), 0)
    cols = lax.broadcasted_iota(jnp.int32, (width, width), 1)
    h = (h_ref[0], h_ref[1])
    t0s, t1s, ps = [], [], []
    for j in range(group):
        k = step * group + j
        top, left = corners[0, k], corners[1, k]
        low_r, low_c = rows >= top, cols >= left

        def cells(ch):
            upper = jnp.where(low_c, obj[ch, :width, :width], obj[ch, :width, width:])
            lower = jnp.where(low_c, obj[ch, width:, :width], obj[ch, width:, width:])
            return jnp.where(low_r, upper, lower).astype(jnp.bfloat16).astype(jnp.float32)

        def turned(ch):
            moved = pltpu.roll(probe[ch], lax.rem(top, width), 0)
            return pltpu.roll(moved, lax.rem(left, width), 1)

        t0s.append((cells(0), cells(1)))
        t1s.append((cells(2), cells(3)))
        ps.append((turned(0), turned(1)))
    wave = [times(p, t) for p, t in zip(ps, t0s)]
    spectrum = transform(wave, tables, False, width)
    inc = transform([times(h, s) for s in spectrum], tables, True, width)
    far = transform([times(t, w) for t, w in zip(t1s, inc)], tables, False, width)
    for j in range(group):
        k = step * group + j
        for c in range(2):
            t1_ref[k, c] = t1s[j][c]
            p_ref[k, c] = ps[j][c]
            inc_ref[k, c] = inc[j][c]
            far_ref[k, c] = far[j][c]


def backward(step, entries, amp, tables, scratch, grads, width):
    h_ref, t1_ref, p_ref, inc_ref, far_ref = scratch
    h = (h_ref[0], h_ref[1])
    damped, t1s = [], []
    for j in range(group):
        k = step * group + j
        far = (far_ref[k, 0], far_ref[k, 1])
        value = amp[entries(k)].astype(jnp.float32)
        factor = 1.0 - value * lax.rsqrt(far[0] * far[0] + far[1] * far[1] + 1.0)
        damped.append((far[0] * factor, far[1] * factor))
        t1s.append((t1_ref[k, 0], t1_ref[k, 1]))
    back = transform(damped, tables, True, width)
    for j in range(group):
        k = step * group + j
        g = conj_times((inc_ref[k, 0], inc_ref[k, 1]), back[j])
        grads[k, 2] = g[0].astype(jnp.bfloat16)
        grads[k, 3] = g[1].astype(jnp.bfloat16)
    spectrum = transform(
        [conj_times(t, w) for t, w in zip(t1s, back)], tables, False, width
    )
    back = transform([conj_times(h, s) for s in spectrum], tables, True, width)
    for j in range(group):
        k = step * group + j
        g = conj_times((p_ref[k, 0], p_ref[k, 1]), back[j])
        grads[k, 0] = g[0].astype(jnp.bfloat16)
        grads[k, 1] = g[1].astype(jnp.bfloat16)


def gather_add(block, corners, obj, grads, out, width):
    count, channels = grads.shape[:2]
    start = pl.multiple_of(block * 16, 16)
    rows = lax.broadcasted_iota(jnp.int32, (16, width), 0) + start
    cols = lax.broadcasted_iota(jnp.int32, (16, width), 1)
    totals = [[jnp.zeros((16, width), jnp.float32)] * 4 for _ in range(channels)]
    for k in range(count):
        low_r, low_c = rows >= corners[0, k], cols >= corners[1, k]
        for ch in range(channels):
            g = grads[k, ch, pl.ds(start, 16), :].astype(jnp.float32)
            upper = jnp.where(low_r, g, 0.0)
            lower = g - upper
            upper_left = jnp.where(low_c, upper, 0.0)
            lower_left = jnp.where(low_c, lower, 0.0)
            t = totals[ch]
            totals[ch] = [
                t[0] + upper_left,
                t[1] + (upper - upper_left),
                t[2] + lower_left,
                t[3] + (lower - lower_left),
            ]
    for ch in range(channels):
        for part in range(4):
            at = pl.ds(pl.multiple_of(start + (part // 2) * width, 16), 16)
            side = pl.ds((part % 2) * width, width)
            out[ch, at, side] = obj[ch, at, side] - step_rate * totals[ch][part]


def tile_edges(upd, edges):
    channels, size = upd.shape[0], upd.shape[1]
    for ch in range(channels):
        edges[0, ch : ch + 1, :] = upd[ch, 0:1, :]
        edges[1, ch : ch + 1, :] = upd[ch, size - 1 : size, :]
        edges[2, ch : ch + 1, :] = upd[ch, :, 0:128].T[0:1, :]
        edges[3, ch : ch + 1, :] = upd[ch, :, size - 128 :].T[127:128, :]


def smooth(upd, above, below, before, after, out):
    channels, size = upd.shape[0], upd.shape[1]
    rows = lax.broadcasted_iota(jnp.int32, (size, size), 0)
    cols = lax.broadcasted_iota(jnp.int32, (size, size), 1)

    def column(row):
        return jnp.broadcast_to(row, (128, size)).T[:, 0:1]

    for s in range(channels // 2):
        pair = (2 * s, 2 * s + 1)
        v = [upd[ch] for ch in pair]
        up = [jnp.where(rows == 0, above[ch : ch + 1, :], pltpu.roll(x, 1, 0)) for ch, x in zip(pair, v)]
        down = [
            jnp.where(rows == size - 1, below[ch : ch + 1, :], pltpu.roll(x, size - 1, 0))
            for ch, x in zip(pair, v)
        ]
        left = [
            jnp.where(cols == 0, column(before[ch : ch + 1, :]), pltpu.roll(x, 1, 1))
            for ch, x in zip(pair, v)
        ]
        right = [
            jnp.where(cols == size - 1, column(after[ch : ch + 1, :]), pltpu.roll(x, size - 1, 1))
            for ch, x in zip(pair, v)
        ]
        total = [jnp.zeros_like(v[0]), jnp.zeros_like(v[0])]
        for view in (up, down, left, right):
            d = [view[0] - v[0], view[1] - v[1]]
            weight = lax.rsqrt(1.0 + d[0] * d[0] + d[1] * d[1])
            total = [total[0] + d[0] * weight, total[1] + d[1] * weight]
        for ch, x, t in zip(pair, v, total):
            out[ch] = x + smooth_rate * t


def step_kernel(
    corners, owner, obj_hbm, probe, phase, table_hbm, measured, out,
    obj, table_ref, amp, upd, edges, halos,
    h_ref, t1_ref, p_ref, inc_ref, far_ref, grads,
    local_sem, send_sem, recv_sem, edge_send, edge_recv,
):
    width, count = probe.shape[-1], corners.shape[1]
    columns = measured.shape[0]
    tx, ty = lax.axis_index("tx"), lax.axis_index("ty")
    tile_rows = lax.axis_size("tx")

    load_obj = pltpu.make_async_copy(obj_hbm, obj, local_sem.at[0])
    load_table = pltpu.make_async_copy(table_hbm, table_ref, local_sem.at[1])
    load_own = pltpu.make_async_copy(measured.at[ty], amp.at[ty], local_sem.at[2])
    load_obj.start()
    load_table.start()
    load_own.start()

    halos[...] = jnp.zeros_like(halos)
    barrier = pltpu.get_barrier_semaphore()
    for d in range(1, columns):
        pl.semaphore_signal(
            barrier, inc=1, device_id={"ty": lax.rem(ty + d, columns)}, device_id_type=MESH
        )
    for d in (1, tile_rows - 1):
        pl.semaphore_signal(
            barrier, inc=1, device_id={"tx": lax.rem(tx + d, tile_rows)}, device_id_type=MESH
        )
    h_ref[0] = jnp.cos(phase[...])
    h_ref[1] = jnp.sin(phase[...])
    pl.semaphore_wait(barrier, columns + 1)

    sends = []
    for d in range(1, columns):
        peer = lax.rem(ty + d, columns)
        sends.append(
            pltpu.make_async_remote_copy(
                src_ref=measured.at[peer],
                dst_ref=amp.at[ty],
                send_sem=send_sem.at[d - 1],
                recv_sem=recv_sem.at[d - 1],
                device_id={"ty": peer},
                device_id_type=MESH,
            )
        )
    for send in sends:
        send.start()
    load_obj.wait()
    load_table.wait()
    scratch = (h_ref, t1_ref, p_ref, inc_ref, far_ref)
    tables = [table_ref.at[i] for i in range(4)]

    def entry(k):
        mine = owner[k]

        def same(i, n):
            return n + jnp.where((owner[i] == mine) & (i < k), 1, 0)

        slot = lax.fori_loop(0, count, same, jnp.int32(0), unroll=True)
        return mine, jnp.minimum(slot, amp.shape[1] - 1)

    @pl.loop(0, count // group)
    def _(step):
        forward(step, (corners, obj, probe, [t[...] for t in tables]), scratch, width)

    load_own.wait()
    for send in sends:
        send.wait()

    @pl.loop(0, count // group)
    def _(step):
        backward(step, entry, amp, [t[...] for t in tables], scratch, grads, width)

    @pl.loop(0, width // 16)
    def _(block):
        gather_add(block, corners, obj, grads, upd, width)

    tile_edges(upd, edges)
    moves = []
    for source, slot, axis, here, size, hop in (
        (1, 0, "tx", tx, tile_rows, 1),
        (0, 1, "tx", tx, tile_rows, -1),
        (3, 2, "ty", ty, columns, 1),
        (2, 3, "ty", ty, columns, -1),
    ):
        move = pltpu.make_async_remote_copy(
            src_ref=edges.at[source],
            dst_ref=halos.at[slot],
            send_sem=edge_send.at[slot],
            recv_sem=edge_recv.at[slot],
            device_id={axis: lax.rem(here + hop + size, size)},
            device_id_type=MESH,
        )
        first, last = here == 0, here == size - 1
        at_end, at_start = (last, first) if hop == 1 else (first, last)
        moves.append((move, jnp.logical_not(at_end), jnp.logical_not(at_start)))
    for move, sends_on, _ in moves:
        pl.when(sends_on)(move.start)
    for move, sends_on, receives in moves:
        pl.when(sends_on)(move.wait_send)
        pl.when(receives)(move.wait_recv)
    smooth(upd, halos[0], halos[1], halos[2], halos[3], out)


def per_device(object_init, probe, propagator_phase, measured, corners, owner_column):
    width = probe.shape[-1]
    channels, size = object_init.shape[0], object_init.shape[1]
    count = corners.shape[2]
    columns = measured.shape[2]
    smem = pl.BlockSpec(memory_space=pltpu.SMEM)
    vmem = pl.BlockSpec(memory_space=pltpu.VMEM)
    anywhere = pl.BlockSpec(memory_space=pl.ANY)
    held = pltpu.VMEM((count, 2, width, width), jnp.float32)
    tile = pltpu.VMEM((channels, size, size), jnp.float32)
    edge = pltpu.VMEM((4, channels, size), jnp.float32)
    return pl.pallas_call(
        step_kernel,
        out_shape=jax.ShapeDtypeStruct(object_init.shape, jnp.float32),
        in_specs=[smem, smem, anywhere, vmem, vmem, anywhere, anywhere],
        out_specs=vmem,
        scratch_shapes=[
            tile,
            pltpu.VMEM((4, 2 * width, 2 * width), jnp.bfloat16),
            pltpu.VMEM(measured.shape[2:], jnp.bfloat16),
            tile, edge, edge,
            pltpu.VMEM((2, width, width), jnp.float32),
            held, held, held, held,
            pltpu.VMEM((count, channels, width, width), jnp.bfloat16),
            pltpu.SemaphoreType.DMA((3,)),
            pltpu.SemaphoreType.DMA((columns - 1,)),
            pltpu.SemaphoreType.DMA((columns - 1,)),
            pltpu.SemaphoreType.DMA((4,)),
            pltpu.SemaphoreType.DMA((4,)),
        ],
        compiler_params=pltpu.CompilerParams(
            collective_id=0, has_side_effects=True, vmem_limit_bytes=60 * 1024 * 1024
        ),
    )(corners[0, 0].T, owner_column[0, 0, :, 0], object_init, probe, propagator_phase,
      dft_blocks(width), measured[0, 0])


def solution(mesh):
    placed = (
        P(None, "tx", "ty"),
        P(),
        P(),
        P("tx", "ty", None, None, None, None),
        P("tx", "ty", None, None),
        P("tx", "ty", None, None),
    )
    return jax.shard_map(
        per_device, mesh=mesh, in_specs=placed, out_specs=P(None, "tx", "ty"), check_vma=False
    )
```
